128 devices in a mesh: col: 64 (over y, z, x), row: 2 (over core).
Axes of the slice: x: 4, y: 4, z: 4, core: 2. Of those that a mesh axis runs over, the one named last changes fastest.
Arguments:
- front: float32 [16384, 16384], P('row', 'col'), as said below
- row_map: int32 [128], replicated, may hold values from 0 to 127, each once
Outputs:
- factored: float32 [16384, 16384], P('row', 'col')
- parent_rows: float32 [16384, 16384], P('row', 'col')
The draws below stay inside these ranges and needn't reach their ends.
Inputs may be any that keep to these rules, and one draw needn't show every extreme that they name: front is symmetric and positive definite.
All inputs are finite; a program needn't handle non-finite values.
Results may differ from the reference program's by a relative error of at most 0.0003.
Values sent between devices are 32-bit elements; how exact they have to be, the bound alone decides.
No kernel may reach another device: no remote copies, remote signals or barrier semaphores. Data moves between devices by JAX's collectives and lax.ppermute only.
A program may use at most 192 MiB of HBM per device.

```python
import math
import jax
import jax.numpy as jnp
from jax import lax

F = 16384
B = 128
PANELS = 6
NBLK = 128


def draw_front(key, part):
    key = jax.random.fold_in(key, 11)
    key_sym = jax.random.fold_in(key, 0)
    key_diag = jax.random.fold_in(key, 1)
    key_place = jax.random.fold_in(key, 3)
    entries = jax.random.normal(key_sym, (F, F), jnp.float32)
    side = math.isqrt(F)
    places = jax.random.permutation(key_place, F).astype(jnp.int32)
    grid_x = (places // side).astype(jnp.float32)
    grid_y = (places % side).astype(jnp.float32)
    reach = math.sqrt(4.0 * F / (2.0 * math.pi * PANELS * B))
    distance = jnp.sqrt((grid_x[:, None] - grid_x[None, :]) ** 2 + (grid_y[:, None] - grid_y[None, :]) ** 2)
    kernel = 3.0 * jnp.exp(distance * jnp.float32(-1.0 / reach))
    symmetric = (entries + entries.T) * jnp.float32(0.7071 / math.sqrt(F))
    diag_vals = jax.random.uniform(key_diag, (F,), jnp.float32, 2.5, 5.0)
    row_ids = lax.broadcasted_iota(jnp.int32, (F, F), 0)
    col_ids = lax.broadcasted_iota(jnp.int32, (F, F), 1)
    matrix = kernel + symmetric + jnp.where(row_ids == col_ids, diag_vals[:, None], jnp.float32(0.0))
    return matrix.astype(jnp.float32)


def setup_inputs(seed: int = 0) -> dict:
    streams_of = jax.random.split(jax.random.key(seed), 3)
    return {
        "front": draw_front(jax.random.fold_in(streams_of[2], 71), 0),
        "row_map": jax.random.permutation(streams_of[1], NBLK).astype(jnp.int32),
    }


def reference(front, row_map):
    matrix = front
    row_ids = lax.broadcasted_iota(jnp.int32, (F, 1), 0)
    for panel in range(PANELS):
        pivot_start = panel * B
        pivot_end = pivot_start + B
        cholesky_block = jnp.linalg.cholesky(matrix[pivot_start:pivot_end, pivot_start:pivot_end])
        factor = jax.scipy.linalg.solve_triangular(cholesky_block, matrix[:, pivot_start:pivot_end].T, lower=True).T
        factor = jnp.where(row_ids >= pivot_start, factor, jnp.float32(0.0))
        trailing = factor[pivot_end:]
        product = jnp.dot(trailing, trailing.T, precision=lax.Precision.HIGHEST)
        matrix = matrix.at[pivot_end:, pivot_end:].add(-product)
        matrix = matrix.at[:, pivot_start:pivot_end].set(factor)
        matrix = matrix.at[pivot_start:pivot_end, pivot_end:].set(jnp.float32(0.0))
    col_ids = lax.broadcasted_iota(jnp.int32, (1, F), 1)
    update = jnp.where(col_ids >= PANELS * B, matrix, jnp.float32(0.0))
    parent = jnp.zeros((NBLK, B, F), jnp.float32).at[row_map].set(update.reshape(NBLK, B, F))
    return (matrix, parent.reshape(F, F))
```

```python
import functools

import jax
import jax.numpy as jnp
from jax import lax
from jax.experimental import pallas as pl
from jax.experimental.pallas import tpu as pltpu
from jax.sharding import PartitionSpec as P

B = 128
PANELS = 6
K = B * PANELS
COLS = 64
W = 256
HALF = 64
GROUP = 4
FIRST = 40
HIGHEST = lax.Precision.HIGHEST
VMEM_LIMIT = 56 * 1024 * 1024


def place(c):
    return c // 16, c // 4 % 4, c % 4


def index(y, z, x):
    return y % 4 * 16 + z % 4 * 4 + x % 4


def mirror(c):
    return (3 - c // 16) * 16 + c % 16


def send(x, pairs):
    return lax.ppermute(x, ("col", "row"), [(a[1] * 2 + a[0], b[1] * 2 + b[0]) for a, b in pairs])


def moved(c, axis, distance):
    at = list(place(c))
    at[axis] += distance
    return index(*at)


def spread(x, axis, sources, me):
    got = [
        send(x, [((0, c), (0, moved(c, axis, d))) for c in sources])
        for d in (1, -1, 2)
    ]
    return jnp.where(me == 1, got[0], jnp.where(me == 3, got[1], jnp.where(me == 2, got[2], x)))


def transpose_kernel(a_ref, t_ref):
    t_ref[...] = a_ref[...].T


def transposed_top(front):
    return pl.pallas_call(
        transpose_kernel,
        grid=(PANELS,),
        in_specs=[pl.BlockSpec((B, W), lambda i: (i, 0))],
        out_specs=pl.BlockSpec((W, B), lambda i: (0, i)),
        out_shape=jax.ShapeDtypeStruct((W, K), jnp.float32),
        name="transpose_top",
    )(front)


def dot(a, b):
    return jnp.dot(a, b, precision=HIGHEST, preferred_element_type=jnp.float32)


def solve_kernel(info_ref, blocks_ref, rhs_ref, hi_ref, lo_ref, w_ref, inv_ref, x_ref):
    w_ref[...] = jnp.zeros_like(w_ref)
    for j in range(3):
        w_ref[j * W : (j + 1) * W, j * W : (j + 1) * W] = blocks_ref[j, :W, :]
    w_ref[0:W, W : 2 * W] = blocks_ref[0, W:, :]
    w_ref[W : 2 * W, 2 * W : 3 * W] = blocks_ref[1, W:, :]
    w_ref[0:W, 2 * W : 3 * W] = blocks_ref[2, W:, :]
    for p in range(PANELS):
        w_ref[p * B : (p + 1) * B, K:] = rhs_ref[:, p * B : (p + 1) * B].T
    x_ref[...] = jnp.zeros_like(x_ref)
    sub = lax.broadcasted_iota(jnp.int32, (8, B), 0)
    lane = lax.broadcasted_iota(jnp.int32, (8, B), 1)

    @pl.loop(0, PANELS)
    def _(p):
        rows = pl.ds(pl.multiple_of(p * B, B), B)
        m = [w_ref[pl.ds(pl.multiple_of(p * B + 8 * t, 8), 8), rows] for t in range(16)]
        g = [jnp.where(lane == sub + 8 * t, 1.0, 0.0) for t in range(16)]
        for j in range(B):
            s, k = divmod(j, 8)
            pivot_row = m[s][k : k + 1, :]
            pivot_inv = g[s][k : k + 1, :]
            scale = 1.0 / m[s][k : k + 1, j : j + 1]
            for t in range(s, 16):
                if t == s and k == 7:
                    continue
                f = m[t][:, j : j + 1] * scale
                if t == s:
                    f = jnp.where(sub[:, :1] > k, f, 0.0)
                m[t] = m[t] - f * pivot_row
                g[t] = g[t] - f * pivot_inv
        for t in range(16):
            d = jnp.sum(jnp.where(lane == sub + 8 * t, m[t], 0.0), axis=1, keepdims=True)
            inv_ref[pl.ds(pl.multiple_of(p * B + 8 * t, 8), 8), :] = g[t] * (1.0 / jnp.sqrt(d))
        u = dot(inv_ref[rows, :], w_ref[rows, :])
        w_ref[rows, :] = u

        @pl.loop(p + 1, PANELS)
        def _(q):
            at = pl.ds(pl.multiple_of(q * B, B), B)
            w_ref[at, :] = w_ref[at, :] - dot(w_ref[rows, at].T, w_ref[rows, :])

    col = info_ref[1]

    @pl.when(col < 3)
    def _():
        for p in range(PANELS):
            r = lax.broadcasted_iota(jnp.int32, (B, W), 0) + p * B
            l = lax.broadcasted_iota(jnp.int32, (B, W), 1) + col * W
            w_ref[p * B : (p + 1) * B, K:] = jnp.where(r == l, 1.0, 0.0)

    @pl.loop(0, PANELS)
    def _(i):
        p = PANELS - 1 - i
        rows = pl.ds(pl.multiple_of(p * B, B), B)
        rest = w_ref[rows, K:] - dot(w_ref[rows, :K], x_ref[...])
        x_ref[rows, :] = dot(inv_ref[rows, :].T, rest)

    x = jnp.where(col < 3, -x_ref[...], x_ref[...])
    hi = x.astype(jnp.bfloat16)
    hi_ref[...] = hi
    lo_ref[...] = (x - hi.astype(jnp.float32)).astype(jnp.bfloat16)


def solve(info, blocks, rhs):
    vmem = pl.BlockSpec(memory_space=pltpu.VMEM)
    return pl.pallas_call(
        solve_kernel,
        in_specs=[pl.BlockSpec(memory_space=pltpu.SMEM), vmem, vmem],
        out_specs=[vmem, vmem],
        out_shape=[jax.ShapeDtypeStruct((K, W), jnp.bfloat16)] * 2,
        scratch_shapes=[
            pltpu.VMEM((K, K + W), jnp.float32),
            pltpu.VMEM((K, B), jnp.float32),
            pltpu.VMEM((K, W), jnp.float32),
        ],
        compiler_params=pltpu.CompilerParams(vmem_limit_bytes=VMEM_LIMIT),
        cost_estimate=pl.CostEstimate(flops=8_000_000_000, bytes_accessed=100_000_000, transcendentals=0),
        name="solve",
    )(info, blocks, rhs)


def gathered_block(r, b):
    c = r * (HALF // 2) + b // 2
    return jnp.where(b % 2 == 0, c, (3 - c // 16) * 16 + c % 16)


def block(ref, b):
    return ref.at[pl.ds(pl.multiple_of(b * B, B), B), :]


def update_kernel(leaving, info_ref, map_ref, panel_ref, front_ref, hi_ref, lo_ref, *rest):
    if leaving:
        fact_ref, send1_ref, send2_ref = rest[:3]
        rest = rest[3:]
    else:
        fact_ref, parent_ref = rest[1:3]
        rest = rest[3:]
    list_ref, panel_buf, base_buf, fact_buf, out_buf, in_sem, out_sem = rest
    r, col = info_ref[0], info_ref[1]

    def listed(b, n):
        mine = (map_ref[r * HALF + b] // HALF) == r
        take = jnp.logical_not(mine) if leaving else mine

        @pl.when(take)
        def _():
            list_ref[n] = b

        return n + take.astype(jnp.int32)

    count = lax.fori_loop(0, HALF, listed, jnp.int32(0))
    steps = (count + GROUP - 1) // GROUP

    def reads(step, j):
        slot = step % 2
        b = list_ref[step * GROUP + j]
        at = pl.ds(j * B, B)
        return (
            pltpu.make_async_copy(block(panel_ref, gathered_block(r, b)), panel_buf.at[slot, at, :], in_sem.at[slot, j, 0]),
            pltpu.make_async_copy(block(front_ref, b), base_buf.at[slot, at, :], in_sem.at[slot, j, 1]),
        )

    def each(step, act):
        for j in range(GROUP):

            @pl.when(step * GROUP + j < count)
            def _():
                act(j)

    def start_reads(step):
        def act(j):
            for copy in reads(step, j):
                copy.start()

        each(step, act)

    def wait_reads(step):
        def act(j):
            for copy in reads(step, j):
                copy.wait()

        each(step, act)

    def writes(step, do):
        slot = step % 2

        def act(j):
            n = step * GROUP + j
            b = list_ref[n]
            at = pl.ds(j * B, B)
            do(pltpu.make_async_copy(fact_buf.at[slot, at, :], block(fact_ref, b), out_sem.at[slot, j, 0]))
            source, sem = out_buf.at[slot, at, :], out_sem.at[slot, j, 1]
            if leaving:

                @pl.when(n < FIRST)
                def _():
                    do(pltpu.make_async_copy(source, block(send1_ref, n), sem))

                @pl.when(n >= FIRST)
                def _():
                    do(pltpu.make_async_copy(source, block(send2_ref, n - FIRST), sem))

            else:
                do(pltpu.make_async_copy(source, block(parent_ref, map_ref[r * HALF + b] - r * HALF), sem))

        each(step, act)

    @pl.when(steps > 0)
    def _():
        start_reads(0)

    @pl.loop(0, steps)
    def _(step):
        slot = step % 2

        @pl.when(step + 1 < steps)
        def _():
            start_reads(step + 1)

        wait_reads(step)

        @pl.when(step >= 2)
        def _():
            writes(step - 2, lambda copy: copy.wait())

        a = panel_buf[slot]
        hi = a.astype(jnp.bfloat16)
        lo = (a - hi.astype(jnp.float32)).astype(jnp.bfloat16)
        product = jnp.dot(hi, hi_ref[...], preferred_element_type=jnp.float32)
        product += jnp.dot(hi, lo_ref[...], preferred_element_type=jnp.float32)
        product += jnp.dot(lo, hi_ref[...], preferred_element_type=jnp.float32)
        lane = lax.broadcasted_iota(jnp.int32, (B, W), 1)
        first = jnp.minimum(2 * col + (lane >= B).astype(jnp.int32), PANELS)
        for j in range(GROUP):
            at = slice(j * B, (j + 1) * B)
            b = r * HALF + list_ref[jnp.minimum(step * GROUP + j, HALF - 1)]
            base = jnp.where(col < 3, 0.0, base_buf[slot, at, :])
            value = jnp.where(b >= first, base - product[at, :], 0.0)
            fact_buf[slot, at, :] = value
            out_buf[slot, at, :] = jnp.where(col < 3, 0.0, value)
        writes(step, lambda copy: copy.start())

    @pl.when(steps >= 2)
    def _():
        writes(steps - 2, lambda copy: copy.wait())

    @pl.when(steps >= 1)
    def _():
        writes(steps - 1, lambda copy: copy.wait())


def update(leaving, info, row_map, panel, front, hi, lo, factored=None):
    smem = pl.BlockSpec(memory_space=pltpu.SMEM)
    vmem = pl.BlockSpec(memory_space=pltpu.VMEM)
    hbm = pl.BlockSpec(memory_space=pl.ANY)
    whole = jax.ShapeDtypeStruct(front.shape, jnp.float32)
    if leaving:
        outs = [whole, jax.ShapeDtypeStruct((FIRST * B, W), jnp.float32), jax.ShapeDtypeStruct(((HALF - FIRST) * B, W), jnp.float32)]
        args, aliases = (), {}
    else:
        outs = [whole, whole]
        args, aliases = (factored,), {6: 0}
    return pl.pallas_call(
        functools.partial(update_kernel, leaving),
        in_specs=[smem, smem, hbm, hbm, vmem, vmem] + [hbm] * len(args),
        out_specs=[hbm] * len(outs),
        out_shape=outs,
        input_output_aliases=aliases,
        scratch_shapes=[
            pltpu.SMEM((HALF,), jnp.int32),
            pltpu.VMEM((2, GROUP * B, K), jnp.float32),
            pltpu.VMEM((2, GROUP * B, W), jnp.float32),
            pltpu.VMEM((2, GROUP * B, W), jnp.float32),
            pltpu.VMEM((2, GROUP * B, W), jnp.float32),
            pltpu.SemaphoreType.DMA((2, GROUP, 2)),
            pltpu.SemaphoreType.DMA((2, GROUP, 2)),
        ],
        compiler_params=pltpu.CompilerParams(vmem_limit_bytes=VMEM_LIMIT),
        cost_estimate=pl.CostEstimate(flops=4_800_000_000, bytes_accessed=32_000_000, transcendentals=0),
        name="update_leaving" if leaving else "update_staying",
    )(info, row_map, panel, front, hi, lo, *args)


def place_kernel(info_ref, map_ref, got1_ref, got2_ref, _, parent_ref, buf, in_sem, out_sem):
    r = info_ref[0]

    def each(do):
        def at(b, n):
            to = map_ref[(1 - r) * HALF + b] - r * HALF
            take = (to >= 0) & (to < HALF)

            @pl.when(take)
            def _():
                do(n, to)

            return n + take.astype(jnp.int32)

        lax.fori_loop(0, HALF, at, jnp.int32(0))

    def read(n, do):
        @pl.when(n < FIRST)
        def _():
            do(pltpu.make_async_copy(block(got1_ref, n), buf.at[n], in_sem.at[n]))

        @pl.when(n >= FIRST)
        def _():
            do(pltpu.make_async_copy(block(got2_ref, n - FIRST), buf.at[n], in_sem.at[n]))

    def write(n, to):
        return pltpu.make_async_copy(buf.at[n], block(parent_ref, to), out_sem.at[n])

    def pass_on(n, to):
        read(n, lambda copy: copy.wait())
        write(n, to).start()

    each(lambda n, to: read(n, lambda copy: copy.start()))
    each(pass_on)
    each(lambda n, to: write(n, to).wait())


def place_received(info, row_map, got1, got2, parent):
    smem = pl.BlockSpec(memory_space=pltpu.SMEM)
    hbm = pl.BlockSpec(memory_space=pl.ANY)
    return pl.pallas_call(
        place_kernel,
        in_specs=[smem, smem, hbm, hbm, hbm],
        out_specs=hbm,
        out_shape=jax.ShapeDtypeStruct(parent.shape, jnp.float32),
        input_output_aliases={4: 0},
        scratch_shapes=[
            pltpu.VMEM((HALF, B, W), jnp.float32),
            pltpu.SemaphoreType.DMA((HALF,)),
            pltpu.SemaphoreType.DMA((HALF,)),
        ],
        compiler_params=pltpu.CompilerParams(vmem_limit_bytes=VMEM_LIMIT),
        name="place_received",
    )(info, row_map, got1, got2, parent)


def per_device(front, row_map):
    r, c = lax.axis_index("row"), lax.axis_index("col")
    y, z, x = c // 16, c // 4 % 4, c % 4
    info = jnp.stack([r, c]).astype(jnp.int32)

    top = transposed_top(front)
    cross = send(
        top[B:],
        [((0, k), (int(place(k)[0] >= 2), mirror(k))) for k in range(COLS)],
    )
    down = send(top, [((0, k), (1, k)) for k in range(COLS)])
    mine = jnp.where(r == 0, top, down)
    piece = jnp.where((y >= 2) == (r == 1), mine[:B], cross)
    panel = lax.all_gather(piece, "col", axis=0, tiled=True)

    top, front_top, _ = lax.optimization_barrier((top, front[:K], piece))
    diag = jnp.where(c == 0, front_top[:W], jnp.where(c == 1, front_top[W : 2 * W], front_top[2 * W :]))
    off = jnp.where(c == 0, top[:, W : 2 * W], jnp.where(c == 1, top[:, 2 * W :], front_top[:W]))
    owners = [0, 1, 2]
    diag = spread(diag, 1, owners, z)
    off = spread(off, 0, owners, y)
    diag = spread(diag, 0, [k for k in range(COLS) if place(k)[0] == 0 and k % 4 < 3], y)
    off = spread(off, 1, [k for k in range(COLS) if place(k)[1] == 0 and k % 4 < 3], z)
    own = jnp.concatenate([diag, off], 0)
    near = {0: own}
    for d in (1, -1, 2):
        near[d % 4] = send(own, [((0, k), (0, moved(k, 2, d))) for k in range(COLS) if k % 4 < 3])
    blocks = []
    for j in range(3):
        d = (x - j) % 4
        blocks.append(jnp.where(d == 0, near[0], jnp.where(d == 1, near[1], jnp.where(d == 2, near[2], near[3]))))
    blocks = jnp.stack(blocks)
    blocks_down = send(blocks, [((0, k), (1, k)) for k in range(COLS)])
    blocks = jnp.where(r == 0, blocks, blocks_down)
    hi, lo = solve(info, blocks, mine)

    factored, send1, send2 = update(True, info, row_map, panel, front, hi, lo)
    swap = [((i, k), (1 - i, k)) for i in range(2) for k in range(COLS)]
    got1 = send(send1, swap)
    factored, parent = update(False, info, row_map, panel, front, hi, lo, factored)
    many = jnp.sum((row_map[:HALF] >= HALF).astype(jnp.int32)) > FIRST
    got2 = lax.cond(many, lambda v: send(v, swap), lambda v: v, send2)
    parent = place_received(info, row_map, got1, got2, parent)
    return factored, parent


def solution(mesh):
    return jax.shard_map(
        per_device,
        mesh=mesh,
        in_specs=(P("row", "col"), P()),
        out_specs=(P("row", "col"), P("row", "col")),
        check_vma=False,
    )
```

```python
import functools

import jax
import jax.numpy as jnp
from jax import lax
from jax.experimental import pallas as pl
from jax.experimental.pallas import tpu as pltpu
from jax.sharding import PartitionSpec as P

B = 128
PANELS = 6
K = B * PANELS
COLS = 64
W = 256
HALF = 64
GROUP = 4
SLOTS = 4
FIRST = 40
HIGHEST = lax.Precision.HIGHEST
VMEM_LIMIT = 56 * 1024 * 1024


def place(c):
    return c // 16, c // 4 % 4, c % 4


def index(y, z, x):
    return y % 4 * 16 + z % 4 * 4 + x % 4


def mirror(c):
    return (3 - c // 16) * 16 + c % 16


def send(x, pairs):
    return lax.ppermute(x, ("col", "row"), [(a[1] * 2 + a[0], b[1] * 2 + b[0]) for a, b in pairs])


def moved(c, axis, distance):
    at = list(place(c))
    at[axis] += distance
    return index(*at)


def spread(x, axis, sources, me):
    got = [
        send(x, [((0, c), (0, moved(c, axis, d))) for c in sources])
        for d in (1, -1, 2)
    ]
    return jnp.where(me == 1, got[0], jnp.where(me == 3, got[1], jnp.where(me == 2, got[2], x)))


def transpose_kernel(a_ref, t_ref, half_ref):
    t = a_ref[...].T
    t_ref[...] = t
    half_ref[...] = t[B:]


def transposed_top(front):
    return pl.pallas_call(
        transpose_kernel,
        grid=(1,),
        in_specs=[pl.BlockSpec((K, W), lambda i: (0, 0))],
        out_specs=[pl.BlockSpec((W, K), lambda i: (0, 0)), pl.BlockSpec((B, K), lambda i: (0, 0))],
        out_shape=[jax.ShapeDtypeStruct((W, K), jnp.float32), jax.ShapeDtypeStruct((B, K), jnp.float32)],
        name="transpose_top",
    )(front)


def dot(a, b):
    return jnp.dot(a, b, precision=HIGHEST, preferred_element_type=jnp.float32)


def eliminate(m, g, sub, inv_ref, p):
    lane = lax.broadcasted_iota(jnp.int32, (8, B), 1)
    for s in range(16):
        j0 = 8 * s
        c = [jnp.broadcast_to(m[s][:, j0 + i : j0 + i + 1], (8, B)) for i in range(8)]
        rows, gows, coef = [], [], []
        for k in range(8):
            scale = 1.0 / c[k][k : k + 1, :]
            row = m[s][k : k + 1, :] * scale
            gow = g[s][k : k + 1, :] * scale
            co = {i: c[i][k : k + 1, :] * scale for i in range(k + 1, 8)}
            rows.append(row)
            gows.append(gow)
            coef.append(co)
            if k < 7:
                f = jnp.where(sub > k, c[k], 0.0)
                for i in range(k + 1, 8):
                    c[i] = c[i] - f * co[i]
                m[s] = m[s] - f * row
                g[s] = g[s] - f * gow
        for t in range(s + 1, 16):
            f = [jnp.broadcast_to(m[t][:, j0 + i : j0 + i + 1], (8, B)) for i in range(8)]
            for k in range(8):
                for i in range(k + 1, 8):
                    f[i] = f[i] - f[k] * coef[k][i]
                m[t] = m[t] - f[k] * rows[k]
                g[t] = g[t] - f[k] * gows[k]
    for t in range(16):
        d = jnp.sum(jnp.where(lane == sub + 8 * t, m[t], 0.0), axis=1, keepdims=True)
        inv_ref[pl.ds(pl.multiple_of(p * B + 8 * t, 8), 8), :] = g[t] * (1.0 / jnp.sqrt(d))


def solve_kernel(info_ref, blocks_ref, rhs_ref, hi_ref, lo_ref, w_ref, inv_ref, x_ref):
    for j in range(3):
        w_ref[j * W : (j + 1) * W, j * W : (j + 1) * W] = blocks_ref[j, :W, :]
    w_ref[0:W, W : 2 * W] = blocks_ref[0, W:, :]
    w_ref[W : 2 * W, 2 * W : 3 * W] = blocks_ref[1, W:, :]
    w_ref[0:W, 2 * W : 3 * W] = blocks_ref[2, W:, :]
    for p in range(PANELS):
        w_ref[p * B : (p + 1) * B, K:] = rhs_ref[:, p * B : (p + 1) * B].T
    sub = lax.broadcasted_iota(jnp.int32, (8, B), 0)
    lane = lax.broadcasted_iota(jnp.int32, (8, B), 1)

    @pl.loop(0, PANELS)
    def _(p):
        at = pl.ds(pl.multiple_of(p * B, B), B)
        m = [w_ref[pl.ds(pl.multiple_of(p * B + 8 * t, 8), 8), at] for t in range(16)]
        g = [jnp.where(lane == sub + 8 * t, 1.0, 0.0) for t in range(16)]
        eliminate(m, g, sub, inv_ref, p)
        for q in range(PANELS):

            @pl.when(p == q)
            def _():
                rows = slice(q * B, (q + 1) * B)
                e = (q + 1) * B
                u = dot(inv_ref[rows, :], w_ref[rows, e:])
                w_ref[rows, e:] = u
                if e < K:
                    w_ref[e:K, e:] = w_ref[e:K, e:] - dot(u[:, : K - e].T, u)

    col = info_ref[1]

    @pl.when(col < 3)
    def _():
        for p in range(PANELS):
            r = lax.broadcasted_iota(jnp.int32, (B, W), 0) + p * B
            l = lax.broadcasted_iota(jnp.int32, (B, W), 1) + col * W
            w_ref[p * B : (p + 1) * B, K:] = jnp.where(r == l, 1.0, 0.0)
    for p in reversed(range(PANELS)):
        rows = slice(p * B, (p + 1) * B)
        e = (p + 1) * B
        rest = w_ref[rows, K:]
        if e < K:
            rest = rest - dot(w_ref[rows, e:K], x_ref[e:, :])
        x_ref[rows, :] = dot(inv_ref[rows, :].T, rest)

    x = jnp.where(col < 3, -x_ref[...], x_ref[...])
    hi = x.astype(jnp.bfloat16)
    hi_ref[...] = hi
    lo_ref[...] = (x - hi.astype(jnp.float32)).astype(jnp.bfloat16)


def solve(info, blocks, rhs):
    vmem = pl.BlockSpec(memory_space=pltpu.VMEM)
    return pl.pallas_call(
        solve_kernel,
        in_specs=[pl.BlockSpec(memory_space=pltpu.SMEM), vmem, vmem],
        out_specs=[vmem, vmem],
        out_shape=[jax.ShapeDtypeStruct((K, W), jnp.bfloat16)] * 2,
        scratch_shapes=[
            pltpu.VMEM((K, K + W), jnp.float32),
            pltpu.VMEM((K, B), jnp.float32),
            pltpu.VMEM((K, W), jnp.float32),
        ],
        compiler_params=pltpu.CompilerParams(vmem_limit_bytes=VMEM_LIMIT),
        cost_estimate=pl.CostEstimate(flops=8_000_000_000, bytes_accessed=100_000_000, transcendentals=0),
        name="solve",
    )(info, blocks, rhs)


def gathered_block(r, b):
    c = r * (HALF // 2) + b // 2
    return jnp.where(b % 2 == 0, c, (3 - c // 16) * 16 + c % 16)


def block(ref, b):
    return ref.at[pl.ds(pl.multiple_of(b * B, B), B), :]


def update_kernel(leaving, info_ref, map_ref, panel_ref, front_ref, hi_ref, lo_ref, *rest):
    if leaving:
        fact_ref, send1_ref, send2_ref = rest[:3]
        rest = rest[3:]
    else:
        fact_ref, parent_ref = rest[1:3]
        rest = rest[3:]
    list_ref, panel_buf, base_buf, fact_buf, out_buf, in_sem, out_sem = rest
    r, col = info_ref[0], info_ref[1]

    def listed(b, n):
        mine = (map_ref[r * HALF + b] // HALF) == r
        take = jnp.logical_not(mine) if leaving else mine

        @pl.when(take)
        def _():
            list_ref[n] = b

        return n + take.astype(jnp.int32)

    count = lax.fori_loop(0, HALF, listed, jnp.int32(0))
    steps = (count + GROUP - 1) // GROUP

    def reads(step, j):
        slot = step % SLOTS
        b = list_ref[step * GROUP + j]
        at = pl.ds(j * B, B)
        return (
            pltpu.make_async_copy(block(panel_ref, gathered_block(r, b)), panel_buf.at[slot, at, :], in_sem.at[slot, j, 0]),
            pltpu.make_async_copy(block(front_ref, b), base_buf.at[slot, at, :], in_sem.at[slot, j, 1]),
        )

    def each(step, act):
        for j in range(GROUP):

            @pl.when(step * GROUP + j < count)
            def _():
                act(j)

    def start_reads(step):
        def act(j):
            for copy in reads(step, j):
                copy.start()

        each(step, act)

    def wait_reads(step):
        def act(j):
            for copy in reads(step, j):
                copy.wait()

        each(step, act)

    def writes(step, do):
        slot = step % SLOTS

        def act(j):
            n = step * GROUP + j
            b = list_ref[n]
            at = pl.ds(j * B, B)
            do(pltpu.make_async_copy(fact_buf.at[slot, at, :], block(fact_ref, b), out_sem.at[slot, j, 0]))
            source, sem = out_buf.at[slot, at, :], out_sem.at[slot, j, 1]
            if leaving:

                @pl.when(n < FIRST)
                def _():
                    do(pltpu.make_async_copy(source, block(send1_ref, n), sem))

                @pl.when(n >= FIRST)
                def _():
                    do(pltpu.make_async_copy(source, block(send2_ref, n - FIRST), sem))

            else:
                do(pltpu.make_async_copy(source, block(parent_ref, map_ref[r * HALF + b] - r * HALF), sem))

        each(step, act)

    for ahead in range(SLOTS - 1):

        @pl.when(ahead < steps)
        def _():
            start_reads(ahead)

    @pl.loop(0, steps)
    def _(step):
        slot = step % SLOTS

        @pl.when(step + SLOTS - 1 < steps)
        def _():
            start_reads(step + SLOTS - 1)

        wait_reads(step)

        @pl.when(step >= SLOTS)
        def _():
            writes(step - SLOTS, lambda copy: copy.wait())

        a = panel_buf[slot]
        hi = a.astype(jnp.bfloat16)
        lo = (a - hi.astype(jnp.float32)).astype(jnp.bfloat16)
        product = jnp.dot(hi, hi_ref[...], preferred_element_type=jnp.float32)
        product += jnp.dot(hi, lo_ref[...], preferred_element_type=jnp.float32)
        product += jnp.dot(lo, hi_ref[...], preferred_element_type=jnp.float32)
        lane = lax.broadcasted_iota(jnp.int32, (B, W), 1)
        first = jnp.minimum(2 * col + (lane >= B).astype(jnp.int32), PANELS)
        for j in range(GROUP):
            at = slice(j * B, (j + 1) * B)
            b = r * HALF + list_ref[jnp.minimum(step * GROUP + j, HALF - 1)]
            base = jnp.where(col < 3, 0.0, base_buf[slot, at, :])
            value = jnp.where(b >= first, base - product[at, :], 0.0)
            fact_buf[slot, at, :] = value
            out_buf[slot, at, :] = jnp.where(col < 3, 0.0, value)
        writes(step, lambda copy: copy.start())

    for behind in range(SLOTS, 0, -1):

        @pl.when(steps >= behind)
        def _():
            writes(steps - behind, lambda copy: copy.wait())


def update(leaving, info, row_map, panel, front, hi, lo, factored=None):
    smem = pl.BlockSpec(memory_space=pltpu.SMEM)
    vmem = pl.BlockSpec(memory_space=pltpu.VMEM)
    hbm = pl.BlockSpec(memory_space=pl.ANY)
    whole = jax.ShapeDtypeStruct(front.shape, jnp.float32)
    if leaving:
        outs = [whole, jax.ShapeDtypeStruct((FIRST * B, W), jnp.float32), jax.ShapeDtypeStruct(((HALF - FIRST) * B, W), jnp.float32)]
        args, aliases = (), {}
    else:
        outs = [whole, whole]
        args, aliases = (factored,), {6: 0}
    return pl.pallas_call(
        functools.partial(update_kernel, leaving),
        in_specs=[smem, smem, hbm, hbm, vmem, vmem] + [hbm] * len(args),
        out_specs=[hbm] * len(outs),
        out_shape=outs,
        input_output_aliases=aliases,
        scratch_shapes=[
            pltpu.SMEM((HALF,), jnp.int32),
            pltpu.VMEM((SLOTS, GROUP * B, K), jnp.float32),
            pltpu.VMEM((SLOTS, GROUP * B, W), jnp.float32),
            pltpu.VMEM((SLOTS, GROUP * B, W), jnp.float32),
            pltpu.VMEM((SLOTS, GROUP * B, W), jnp.float32),
            pltpu.SemaphoreType.DMA((SLOTS, GROUP, 2)),
            pltpu.SemaphoreType.DMA((SLOTS, GROUP, 2)),
        ],
        compiler_params=pltpu.CompilerParams(vmem_limit_bytes=VMEM_LIMIT),
        cost_estimate=pl.CostEstimate(flops=4_800_000_000, bytes_accessed=32_000_000, transcendentals=0),
        name="update_leaving" if leaving else "update_staying",
    )(info, row_map, panel, front, hi, lo, *args)


def place_kernel(info_ref, map_ref, got1_ref, got2_ref, _, parent_ref, buf, in_sem, out_sem):
    r = info_ref[0]

    def each(do):
        def at(b, n):
            to = map_ref[(1 - r) * HALF + b] - r * HALF
            take = (to >= 0) & (to < HALF)

            @pl.when(take)
            def _():
                do(n, to)

            return n + take.astype(jnp.int32)

        lax.fori_loop(0, HALF, at, jnp.int32(0))

    def read(n, do):
        @pl.when(n < FIRST)
        def _():
            do(pltpu.make_async_copy(block(got1_ref, n), buf.at[n], in_sem.at[n]))

        @pl.when(n >= FIRST)
        def _():
            do(pltpu.make_async_copy(block(got2_ref, n - FIRST), buf.at[n], in_sem.at[n]))

    def write(n, to):
        return pltpu.make_async_copy(buf.at[n], block(parent_ref, to), out_sem.at[n])

    def pass_on(n, to):
        read(n, lambda copy: copy.wait())
        write(n, to).start()

    each(lambda n, to: read(n, lambda copy: copy.start()))
    each(pass_on)
    each(lambda n, to: write(n, to).wait())


def place_received(info, row_map, got1, got2, parent):
    smem = pl.BlockSpec(memory_space=pltpu.SMEM)
    hbm = pl.BlockSpec(memory_space=pl.ANY)
    return pl.pallas_call(
        place_kernel,
        in_specs=[smem, smem, hbm, hbm, hbm],
        out_specs=hbm,
        out_shape=jax.ShapeDtypeStruct(parent.shape, jnp.float32),
        input_output_aliases={4: 0},
        scratch_shapes=[
            pltpu.VMEM((HALF, B, W), jnp.float32),
            pltpu.SemaphoreType.DMA((HALF,)),
            pltpu.SemaphoreType.DMA((HALF,)),
        ],
        compiler_params=pltpu.CompilerParams(vmem_limit_bytes=VMEM_LIMIT),
        name="place_received",
    )(info, row_map, got1, got2, parent)


def per_device(front, row_map):
    r, c = lax.axis_index("row"), lax.axis_index("col")
    y, z, x = c // 16, c // 4 % 4, c % 4
    info = jnp.stack([r, c]).astype(jnp.int32)

    top, top_half = transposed_top(front)
    cross = send(
        top_half,
        [((0, k), (int(place(k)[0] >= 2), mirror(k))) for k in range(COLS)],
    )
    down = send(top, [((0, k), (1, k)) for k in range(COLS)])
    mine = jnp.where(r == 0, top, down)
    piece = jnp.where((y >= 2) == (r == 1), mine[:B], cross)
    panel = lax.all_gather(piece, "col", axis=0, tiled=True)

    top, front_top, _ = lax.optimization_barrier((top, front[:K], piece))
    diag = jnp.where(c == 0, front_top[:W], jnp.where(c == 1, front_top[W : 2 * W], front_top[2 * W :]))
    off = jnp.where(c == 0, top[:, W : 2 * W], jnp.where(c == 1, top[:, 2 * W :], front_top[:W]))
    owners = [0, 1, 2]
    diag = spread(diag, 1, owners, z)
    off = spread(off, 0, owners, y)
    diag = spread(diag, 0, [k for k in range(COLS) if place(k)[0] == 0 and k % 4 < 3], y)
    off = spread(off, 1, [k for k in range(COLS) if place(k)[1] == 0 and k % 4 < 3], z)
    own = jnp.concatenate([diag, off], 0)
    near = {0: own}
    for d in (1, -1, 2):
        near[d % 4] = send(own, [((0, k), (0, moved(k, 2, d))) for k in range(COLS) if k % 4 < 3])
    blocks = []
    for j in range(3):
        d = (x - j) % 4
        blocks.append(jnp.where(d == 0, near[0], jnp.where(d == 1, near[1], jnp.where(d == 2, near[2], near[3]))))
    blocks = jnp.stack(blocks)
    blocks_down = send(blocks, [((0, k), (1, k)) for k in range(COLS)])
    blocks = jnp.where(r == 0, blocks, blocks_down)
    hi, lo = solve(info, blocks, mine)

    factored, send1, send2 = update(True, info, row_map, panel, front, hi, lo)
    swap = [((i, k), (1 - i, k)) for i in range(2) for k in range(COLS)]
    got1 = send(send1, swap)
    factored, parent = update(False, info, row_map, panel, front, hi, lo, factored)
    many = jnp.sum((row_map[:HALF] >= HALF).astype(jnp.int32)) > FIRST
    got2 = lax.cond(many, lambda v: send(v, swap), lambda v: v, send2)
    parent = place_received(info, row_map, got1, got2, parent)
    return factored, parent


def solution(mesh):
    return jax.shard_map(
        per_device,
        mesh=mesh,
        in_specs=(P("row", "col"), P()),
        out_specs=(P("row", "col"), P("row", "col")),
        check_vma=False,
    )
```

```python
import functools

import jax
import jax.numpy as jnp
from jax import lax
from jax.experimental import pallas as pl
from jax.experimental.pallas import tpu as pltpu
from jax.sharding import PartitionSpec as P

B = 128
PANELS = 6
K = B * PANELS
COLS = 64
W = 256
HALF = 64
GROUP = 4
SLOTS = 4
FIRST = 40
HIGHEST = lax.Precision.HIGHEST
VMEM_LIMIT = 56 * 1024 * 1024


def place(c):
    return c // 16, c // 4 % 4, c % 4


def index(y, z, x):
    return y % 4 * 16 + z % 4 * 4 + x % 4


def mirror(c):
    return (3 - c // 16) * 16 + c % 16


def send(x, pairs):
    return lax.ppermute(x, ("col", "row"), [(a[1] * 2 + a[0], b[1] * 2 + b[0]) for a, b in pairs])


def moved(c, axis, distance):
    at = list(place(c))
    at[axis] += distance
    return index(*at)


def spread(x, axis, sources, me):
    up = send(x, [((0, c), (0, moved(c, axis, 1))) for c in sources])
    down = send(x, [((0, c), (0, moved(c, axis, -1))) for c in sources])
    far = send(up, [((0, moved(c, axis, 1)), (0, moved(c, axis, 2))) for c in sources])
    return jnp.where(me == 1, up, jnp.where(me == 3, down, jnp.where(me == 2, far, x)))


def transpose_kernel(a_ref, t_ref, half_ref):
    t = a_ref[...].T
    t_ref[...] = t
    half_ref[...] = t[B:]


def transposed_top(front):
    return pl.pallas_call(
        transpose_kernel,
        grid=(1,),
        in_specs=[pl.BlockSpec((K, W), lambda i: (0, 0))],
        out_specs=[pl.BlockSpec((W, K), lambda i: (0, 0)), pl.BlockSpec((B, K), lambda i: (0, 0))],
        out_shape=[jax.ShapeDtypeStruct((W, K), jnp.float32), jax.ShapeDtypeStruct((B, K), jnp.float32)],
        name="transpose_top",
    )(front)


def dot(a, b):
    return jnp.dot(a, b, precision=HIGHEST, preferred_element_type=jnp.float32)


def eliminate(m, g, sub, inv_ref, p):
    lane = lax.broadcasted_iota(jnp.int32, (8, B), 1)
    for s in range(16):
        j0 = 8 * s
        c = [jnp.broadcast_to(m[s][:, j0 + i : j0 + i + 1], (8, B)) for i in range(8)]
        rows, gows, coef = [], [], []
        for k in range(8):
            scale = 1.0 / c[k][k : k + 1, :]
            row = m[s][k : k + 1, :] * scale
            gow = g[s][k : k + 1, :] * scale
            co = {i: c[i][k : k + 1, :] * scale for i in range(k + 1, 8)}
            rows.append(row)
            gows.append(gow)
            coef.append(co)
            if k < 7:
                f = jnp.where(sub > k, c[k], 0.0)
                for i in range(k + 1, 8):
                    c[i] = c[i] - f * co[i]
                m[s] = m[s] - f * row
                g[s] = g[s] - f * gow
        for t in range(s + 1, 16):
            f = [jnp.broadcast_to(m[t][:, j0 + i : j0 + i + 1], (8, B)) for i in range(8)]
            for k in range(8):
                for i in range(k + 1, 8):
                    f[i] = f[i] - f[k] * coef[k][i]
                m[t] = m[t] - f[k] * rows[k]
                g[t] = g[t] - f[k] * gows[k]
    for t in range(16):
        d = jnp.sum(jnp.where(lane == sub + 8 * t, m[t], 0.0), axis=1, keepdims=True)
        inv_ref[pl.ds(pl.multiple_of(p * B + 8 * t, 8), 8), :] = g[t] * (1.0 / jnp.sqrt(d))


def plan(info_ref, map_ref, plan_ref):
    r = info_ref[0]

    def at(b, counts):
        leaving, staying, coming = counts
        leaves = (map_ref[r * HALF + b] // HALF != r).astype(jnp.int32)
        to = map_ref[(1 - r) * HALF + b]
        comes = (to // HALF == r).astype(jnp.int32)
        plan_ref[jnp.where(leaves == 1, leaving, HALF + staying)] = b

        @pl.when(comes == 1)
        def _():
            plan_ref[2 * HALF + coming] = to - r * HALF

        return leaving + leaves, staying + 1 - leaves, coming + comes

    counts = lax.fori_loop(0, HALF, at, (jnp.int32(0),) * 3)
    for i, count in enumerate(counts):
        plan_ref[3 * HALF + i] = count


def solve_kernel(info_ref, map_ref, blocks_ref, rhs_ref, hi_ref, lo_ref, plan_ref, w_ref, inv_ref, x_ref):
    plan(info_ref, map_ref, plan_ref)
    for j in range(3):
        w_ref[j * W : (j + 1) * W, j * W : (j + 1) * W] = blocks_ref[j, :W, :]
    w_ref[0:W, W : 2 * W] = blocks_ref[0, W:, :]
    w_ref[W : 2 * W, 2 * W : 3 * W] = blocks_ref[1, W:, :]
    w_ref[0:W, 2 * W : 3 * W] = blocks_ref[2, W:, :]
    for p in range(PANELS):
        w_ref[p * B : (p + 1) * B, K:] = rhs_ref[:, p * B : (p + 1) * B].T
    sub = lax.broadcasted_iota(jnp.int32, (8, B), 0)
    lane = lax.broadcasted_iota(jnp.int32, (8, B), 1)

    @pl.loop(0, PANELS)
    def _(p):
        at = pl.ds(pl.multiple_of(p * B, B), B)
        m = [w_ref[pl.ds(pl.multiple_of(p * B + 8 * t, 8), 8), at] for t in range(16)]
        g = [jnp.where(lane == sub + 8 * t, 1.0, 0.0) for t in range(16)]
        eliminate(m, g, sub, inv_ref, p)
        for q in range(PANELS):

            @pl.when(p == q)
            def _():
                rows = slice(q * B, (q + 1) * B)
                e = (q + 1) * B
                u = dot(inv_ref[rows, :], w_ref[rows, e:])
                w_ref[rows, e:] = u
                if e < K:
                    w_ref[e:K, e:] = w_ref[e:K, e:] - dot(u[:, : K - e].T, u)

    col = info_ref[1]

    @pl.when(col < 3)
    def _():
        for p in range(PANELS):
            r = lax.broadcasted_iota(jnp.int32, (B, W), 0) + p * B
            l = lax.broadcasted_iota(jnp.int32, (B, W), 1) + col * W
            w_ref[p * B : (p + 1) * B, K:] = jnp.where(r == l, 1.0, 0.0)
    for p in reversed(range(PANELS)):
        rows = slice(p * B, (p + 1) * B)
        e = (p + 1) * B
        rest = w_ref[rows, K:]
        if e < K:
            rest = rest - dot(w_ref[rows, e:K], x_ref[e:, :])
        x_ref[rows, :] = dot(inv_ref[rows, :].T, rest)

    x = jnp.where(col < 3, -x_ref[...], x_ref[...])
    hi = x.astype(jnp.bfloat16)
    hi_ref[...] = hi
    lo_ref[...] = (x - hi.astype(jnp.float32)).astype(jnp.bfloat16)


def solve(info, row_map, blocks, rhs):
    vmem = pl.BlockSpec(memory_space=pltpu.VMEM)
    smem = pl.BlockSpec(memory_space=pltpu.SMEM)
    return pl.pallas_call(
        solve_kernel,
        in_specs=[smem, smem, vmem, vmem],
        out_specs=[vmem, vmem, smem],
        out_shape=[jax.ShapeDtypeStruct((K, W), jnp.bfloat16)] * 2 + [jax.ShapeDtypeStruct((4 * HALF,), jnp.int32)],
        scratch_shapes=[
            pltpu.VMEM((K, K + W), jnp.float32),
            pltpu.VMEM((K, B), jnp.float32),
            pltpu.VMEM((K, W), jnp.float32),
        ],
        compiler_params=pltpu.CompilerParams(vmem_limit_bytes=VMEM_LIMIT),
        cost_estimate=pl.CostEstimate(flops=8_000_000_000, bytes_accessed=100_000_000, transcendentals=0),
        name="solve",
    )(info, row_map, blocks, rhs)


def gathered_block(r, b):
    c = r * (HALF // 2) + b // 2
    return jnp.where(b % 2 == 0, c, (3 - c // 16) * 16 + c % 16)


def block(ref, b):
    return ref.at[pl.ds(pl.multiple_of(b * B, B), B), :]


def update_kernel(leaving, info_ref, map_ref, plan_ref, panel_ref, front_ref, hi_ref, lo_ref, *rest):
    if leaving:
        fact_ref, send1_ref, send2_ref = rest[:3]
        rest = rest[3:]
    else:
        fact_ref, parent_ref = rest[1:3]
        rest = rest[3:]
    panel_buf, base_buf, fact_buf, out_buf, in_sem, out_sem = rest
    r, col = info_ref[0], info_ref[1]

    first_entry = 0 if leaving else HALF
    count = plan_ref[3 * HALF + (0 if leaving else 1)]
    steps = (count + GROUP - 1) // GROUP

    def reads(step, j):
        slot = step % SLOTS
        b = plan_ref[first_entry + step * GROUP + j]
        at = pl.ds(j * B, B)
        return (
            pltpu.make_async_copy(block(panel_ref, gathered_block(r, b)), panel_buf.at[slot, at, :], in_sem.at[slot, j, 0]),
            pltpu.make_async_copy(block(front_ref, b), base_buf.at[slot, at, :], in_sem.at[slot, j, 1]),
        )

    def each(step, act):
        for j in range(GROUP):

            @pl.when(step * GROUP + j < count)
            def _():
                act(j)

    def start_reads(step):
        def act(j):
            for copy in reads(step, j):
                copy.start()

        each(step, act)

    def wait_reads(step):
        def act(j):
            for copy in reads(step, j):
                copy.wait()

        each(step, act)

    def writes(step, do):
        slot = step % SLOTS

        def act(j):
            n = step * GROUP + j
            b = plan_ref[first_entry + n]
            at = pl.ds(j * B, B)
            do(pltpu.make_async_copy(fact_buf.at[slot, at, :], block(fact_ref, b), out_sem.at[slot, j, 0]))
            source, sem = out_buf.at[slot, at, :], out_sem.at[slot, j, 1]
            if leaving:

                @pl.when(n < FIRST)
                def _():
                    do(pltpu.make_async_copy(source, block(send1_ref, n), sem))

                @pl.when(n >= FIRST)
                def _():
                    do(pltpu.make_async_copy(source, block(send2_ref, n - FIRST), sem))

            else:
                do(pltpu.make_async_copy(source, block(parent_ref, map_ref[r * HALF + b] - r * HALF), sem))

        each(step, act)

    for ahead in range(SLOTS - 1):

        @pl.when(ahead < steps)
        def _():
            start_reads(ahead)

    @pl.loop(0, steps)
    def _(step):
        slot = step % SLOTS

        @pl.when(step + SLOTS - 1 < steps)
        def _():
            start_reads(step + SLOTS - 1)

        wait_reads(step)

        @pl.when(step >= SLOTS)
        def _():
            writes(step - SLOTS, lambda copy: copy.wait())

        a = panel_buf[slot]
        hi = a.astype(jnp.bfloat16)
        lo = (a - hi.astype(jnp.float32)).astype(jnp.bfloat16)
        product = jnp.dot(hi, hi_ref[...], preferred_element_type=jnp.float32)
        product += jnp.dot(hi, lo_ref[...], preferred_element_type=jnp.float32)
        product += jnp.dot(lo, hi_ref[...], preferred_element_type=jnp.float32)
        lane = lax.broadcasted_iota(jnp.int32, (B, W), 1)
        first = jnp.minimum(2 * col + (lane >= B).astype(jnp.int32), PANELS)
        for j in range(GROUP):
            at = slice(j * B, (j + 1) * B)
            b = r * HALF + plan_ref[first_entry + jnp.minimum(step * GROUP + j, count - 1)]
            base = jnp.where(col < 3, 0.0, base_buf[slot, at, :])
            value = jnp.where(b >= first, base - product[at, :], 0.0)
            fact_buf[slot, at, :] = value
            out_buf[slot, at, :] = jnp.where(col < 3, 0.0, value)
        writes(step, lambda copy: copy.start())

    for behind in range(SLOTS, 0, -1):

        @pl.when(steps >= behind)
        def _():
            writes(steps - behind, lambda copy: copy.wait())


def update(leaving, info, row_map, lists, panel, front, hi, lo, factored=None):
    smem = pl.BlockSpec(memory_space=pltpu.SMEM)
    vmem = pl.BlockSpec(memory_space=pltpu.VMEM)
    hbm = pl.BlockSpec(memory_space=pl.ANY)
    whole = jax.ShapeDtypeStruct(front.shape, jnp.float32)
    if leaving:
        outs = [whole, jax.ShapeDtypeStruct((FIRST * B, W), jnp.float32), jax.ShapeDtypeStruct(((HALF - FIRST) * B, W), jnp.float32)]
        args, aliases = (), {}
    else:
        outs = [whole, whole]
        args, aliases = (factored,), {7: 0}
    return pl.pallas_call(
        functools.partial(update_kernel, leaving),
        in_specs=[smem, smem, smem, hbm, hbm, vmem, vmem] + [hbm] * len(args),
        out_specs=[hbm] * len(outs),
        out_shape=outs,
        input_output_aliases=aliases,
        scratch_shapes=[
            pltpu.VMEM((SLOTS, GROUP * B, K), jnp.float32),
            pltpu.VMEM((SLOTS, GROUP * B, W), jnp.float32),
            pltpu.VMEM((SLOTS, GROUP * B, W), jnp.float32),
            pltpu.VMEM((SLOTS, GROUP * B, W), jnp.float32),
            pltpu.SemaphoreType.DMA((SLOTS, GROUP, 2)),
            pltpu.SemaphoreType.DMA((SLOTS, GROUP, 2)),
        ],
        compiler_params=pltpu.CompilerParams(vmem_limit_bytes=VMEM_LIMIT),
        cost_estimate=pl.CostEstimate(flops=4_800_000_000, bytes_accessed=32_000_000, transcendentals=0),
        name="update_leaving" if leaving else "update_staying",
    )(info, row_map, lists, panel, front, hi, lo, *args)


def place_kernel(plan_ref, got1_ref, got2_ref, _, parent_ref, buf, in_sem, out_sem):
    def read1(n):
        return pltpu.make_async_copy(block(got1_ref, n), buf.at[n], in_sem.at[n])

    def read2(n):
        return pltpu.make_async_copy(block(got2_ref, n - FIRST), buf.at[n], in_sem.at[n])

    def write(n):
        return pltpu.make_async_copy(buf.at[n], block(parent_ref, plan_ref[2 * HALF + n]), out_sem.at[n])

    def each(first, last, act):
        @pl.loop(first, last)
        def _(n):
            act(n)

    def pass_on(copy, n):
        copy.wait()
        write(n).start()

    count = plan_ref[3 * HALF + 2]
    split = jnp.minimum(count, FIRST)
    each(0, split, lambda n: read1(n).start())
    each(split, count, lambda n: read2(n).start())
    each(0, split, lambda n: pass_on(read1(n), n))
    each(split, count, lambda n: pass_on(read2(n), n))
    each(0, count, lambda n: write(n).wait())


def place_received(lists, got1, got2, parent):
    smem = pl.BlockSpec(memory_space=pltpu.SMEM)
    hbm = pl.BlockSpec(memory_space=pl.ANY)
    return pl.pallas_call(
        place_kernel,
        in_specs=[smem, hbm, hbm, hbm],
        out_specs=hbm,
        out_shape=jax.ShapeDtypeStruct(parent.shape, jnp.float32),
        input_output_aliases={3: 0},
        scratch_shapes=[
            pltpu.VMEM((HALF, B, W), jnp.float32),
            pltpu.SemaphoreType.DMA((HALF,)),
            pltpu.SemaphoreType.DMA((HALF,)),
        ],
        compiler_params=pltpu.CompilerParams(vmem_limit_bytes=VMEM_LIMIT),
        name="place_received",
    )(lists, got1, got2, parent)


def per_device(front, row_map):
    r, c = lax.axis_index("row"), lax.axis_index("col")
    y, z, x = c // 16, c // 4 % 4, c % 4
    info = jnp.stack([r, c]).astype(jnp.int32)

    top, top_half = transposed_top(front)
    cross = send(
        top_half,
        [((0, k), (int(place(k)[0] >= 2), mirror(k))) for k in range(COLS)],
    )
    down = send(top, [((0, k), (1, k)) for k in range(COLS)])
    mine = jnp.where(r == 0, top, down)
    piece = jnp.where((y >= 2) == (r == 1), mine[:B], cross)
    panel = lax.all_gather(piece, "col", axis=0, tiled=True)

    top, front_top, _ = lax.optimization_barrier((top, front[:K], piece))
    diag = jnp.where(c == 0, front_top[:W], jnp.where(c == 1, front_top[W : 2 * W], front_top[2 * W :]))
    off = jnp.where(c == 0, top[:, W : 2 * W], jnp.where(c == 1, top[:, 2 * W :], front_top[:W]))
    owners = [0, 1, 2]
    diag = spread(diag, 1, owners, z)
    off = spread(off, 0, owners, y)
    diag = spread(diag, 0, [k for k in range(COLS) if place(k)[0] == 0 and k % 4 < 3], y)
    off = spread(off, 1, [k for k in range(COLS) if place(k)[1] == 0 and k % 4 < 3], z)
    own = jnp.concatenate([diag, off], 0)
    near = {0: own}
    for d in (1, -1):
        near[d % 4] = send(own, [((0, k), (0, moved(k, 2, d))) for k in range(COLS) if k % 4 < 3])
    halves = [
        send(near[1][:W], [((0, moved(k, 2, 1)), (0, moved(k, 2, 2))) for k in range(COLS) if k % 4 < 3]),
        send(near[3][W:], [((0, moved(k, 2, -1)), (0, moved(k, 2, -2))) for k in range(COLS) if k % 4 < 3]),
    ]
    near[2] = jnp.concatenate(halves, 0)
    blocks = []
    for j in range(3):
        d = (x - j) % 4
        blocks.append(jnp.where(d == 0, near[0], jnp.where(d == 1, near[1], jnp.where(d == 2, near[2], near[3]))))
    blocks = jnp.stack(blocks)
    blocks_down = send(blocks, [((0, k), (1, k)) for k in range(COLS)])
    blocks = jnp.where(r == 0, blocks, blocks_down)
    hi, lo, lists = solve(info, row_map, blocks, mine)

    factored, send1, send2 = update(True, info, row_map, lists, panel, front, hi, lo)
    swap = [((i, k), (1 - i, k)) for i in range(2) for k in range(COLS)]
    got1 = send(send1, swap)
    factored, parent = update(False, info, row_map, lists, panel, front, hi, lo, factored)
    many = jnp.sum((row_map[:HALF] >= HALF).astype(jnp.int32)) > FIRST
    got2 = lax.cond(many, lambda v: send(v, swap), lambda v: v, send2)
    parent = place_received(lists, got1, got2, parent)
    return factored, parent


def solution(mesh):
    return jax.shard_map(
        per_device,
        mesh=mesh,
        in_specs=(P("row", "col"), P()),
        out_specs=(P("row", "col"), P("row", "col")),
        check_vma=False,
    )
```

```python
import functools

import jax
import jax.numpy as jnp
from jax import lax
from jax.experimental import pallas as pl
from jax.experimental.pallas import tpu as pltpu
from jax.sharding import PartitionSpec as P

B = 128
PANELS = 6
K = B * PANELS
COLS = 64
W = 256
HALF = 64
GROUP = 4
SLOTS = 4
FIRST = 40
CHUNK = 8
HIGHEST = lax.Precision.HIGHEST
VMEM_LIMIT = 56 * 1024 * 1024


def place(c):
    return c // 16, c // 4 % 4, c % 4


def index(y, z, x):
    return y % 4 * 16 + z % 4 * 4 + x % 4


def mirror(c):
    return (3 - c // 16) * 16 + c % 16


def send(x, pairs):
    return lax.ppermute(x, ("col", "row"), [(a[1] * 2 + a[0], b[1] * 2 + b[0]) for a, b in pairs])


def moved(c, axis, distance):
    at = list(place(c))
    at[axis] += distance
    return index(*at)


def spread(x, axis, sources, me):
    up = send(x, [((0, c), (0, moved(c, axis, 1))) for c in sources])
    down = send(x, [((0, c), (0, moved(c, axis, -1))) for c in sources])
    far = send(up, [((0, moved(c, axis, 1)), (0, moved(c, axis, 2))) for c in sources])
    return jnp.where(me == 1, up, jnp.where(me == 3, down, jnp.where(me == 2, far, x)))


def transpose_kernel(a_ref, t_ref, half_ref):
    t = a_ref[...].T
    t_ref[...] = t
    half_ref[...] = t[B:]


def transposed_top(front):
    return pl.pallas_call(
        transpose_kernel,
        grid=(1,),
        in_specs=[pl.BlockSpec((K, W), lambda i: (0, 0))],
        out_specs=[pl.BlockSpec((W, K), lambda i: (0, 0)), pl.BlockSpec((B, K), lambda i: (0, 0))],
        out_shape=[jax.ShapeDtypeStruct((W, K), jnp.float32), jax.ShapeDtypeStruct((B, K), jnp.float32)],
        name="transpose_top",
    )(front)


def dot(a, b):
    return jnp.dot(a, b, precision=HIGHEST, preferred_element_type=jnp.float32)


def eliminate(m, g, sub, inv_ref, p):
    lane = lax.broadcasted_iota(jnp.int32, (8, B), 1)
    for s in range(16):
        j0 = 8 * s
        c = [jnp.broadcast_to(m[s][:, j0 + i : j0 + i + 1], (8, B)) for i in range(8)]
        rows, gows, coef = [], [], []
        for k in range(8):
            scale = 1.0 / c[k][k : k + 1, :]
            row = m[s][k : k + 1, :] * scale
            gow = g[s][k : k + 1, :] * scale
            co = {i: c[i][k : k + 1, :] * scale for i in range(k + 1, 8)}
            rows.append(row)
            gows.append(gow)
            coef.append(co)
            if k < 7:
                f = jnp.where(sub > k, c[k], 0.0)
                for i in range(k + 1, 8):
                    c[i] = c[i] - f * co[i]
                m[s] = m[s] - f * row
                g[s] = g[s] - f * gow
        for t in range(s + 1, 16):
            f = [jnp.broadcast_to(m[t][:, j0 + i : j0 + i + 1], (8, B)) for i in range(8)]
            for k in range(8):
                for i in range(k + 1, 8):
                    f[i] = f[i] - f[k] * coef[k][i]
                m[t] = m[t] - f[k] * rows[k]
                g[t] = g[t] - f[k] * gows[k]
    for t in range(16):
        d = jnp.sum(jnp.where(lane == sub + 8 * t, m[t], 0.0), axis=1, keepdims=True)
        inv_ref[pl.ds(pl.multiple_of(p * B + 8 * t, 8), 8), :] = g[t] * (1.0 / jnp.sqrt(d))


def plan(info_ref, map_ref, plan_ref):
    r = info_ref[0]

    def at(b, counts):
        leaving, staying, coming = counts
        leaves = (map_ref[r * HALF + b] // HALF != r).astype(jnp.int32)
        to = map_ref[(1 - r) * HALF + b]
        comes = (to // HALF == r).astype(jnp.int32)
        plan_ref[jnp.where(leaves == 1, leaving, HALF + staying)] = b

        @pl.when(comes == 1)
        def _():
            plan_ref[2 * HALF + coming] = to - r * HALF

        return leaving + leaves, staying + 1 - leaves, coming + comes

    counts = lax.fori_loop(0, HALF, at, (jnp.int32(0),) * 3)
    for i, count in enumerate(counts):
        plan_ref[3 * HALF + i] = count


def solve_kernel(info_ref, map_ref, blocks_ref, rhs_ref, hi_ref, lo_ref, plan_ref, w_ref, inv_ref, x_ref):
    plan(info_ref, map_ref, plan_ref)
    for j in range(3):
        w_ref[j * W : (j + 1) * W, j * W : (j + 1) * W] = blocks_ref[j, :W, :]
    w_ref[0:W, W : 2 * W] = blocks_ref[0, W:, :]
    w_ref[W : 2 * W, 2 * W : 3 * W] = blocks_ref[1, W:, :]
    w_ref[0:W, 2 * W : 3 * W] = blocks_ref[2, W:, :]
    for p in range(PANELS):
        w_ref[p * B : (p + 1) * B, K:] = rhs_ref[:, p * B : (p + 1) * B].T
    sub = lax.broadcasted_iota(jnp.int32, (8, B), 0)
    lane = lax.broadcasted_iota(jnp.int32, (8, B), 1)

    @pl.loop(0, PANELS)
    def _(p):
        at = pl.ds(pl.multiple_of(p * B, B), B)
        m = [w_ref[pl.ds(pl.multiple_of(p * B + 8 * t, 8), 8), at] for t in range(16)]
        g = [jnp.where(lane == sub + 8 * t, 1.0, 0.0) for t in range(16)]
        eliminate(m, g, sub, inv_ref, p)
        for q in range(PANELS):

            @pl.when(p == q)
            def _():
                rows = slice(q * B, (q + 1) * B)
                e = (q + 1) * B
                u = dot(inv_ref[rows, :], w_ref[rows, e:])
                w_ref[rows, e:] = u
                if e < K:
                    w_ref[e:K, e:] = w_ref[e:K, e:] - dot(u[:, : K - e].T, u)

    col = info_ref[1]

    @pl.when(col < 3)
    def _():
        for p in range(PANELS):
            r = lax.broadcasted_iota(jnp.int32, (B, W), 0) + p * B
            l = lax.broadcasted_iota(jnp.int32, (B, W), 1) + col * W
            w_ref[p * B : (p + 1) * B, K:] = jnp.where(r == l, 1.0, 0.0)
    for p in reversed(range(PANELS)):
        rows = slice(p * B, (p + 1) * B)
        e = (p + 1) * B
        rest = w_ref[rows, K:]
        if e < K:
            rest = rest - dot(w_ref[rows, e:K], x_ref[e:, :])
        x_ref[rows, :] = dot(inv_ref[rows, :].T, rest)

    x = jnp.where(col < 3, -x_ref[...], x_ref[...])
    hi = x.astype(jnp.bfloat16)
    hi_ref[...] = hi
    lo_ref[...] = (x - hi.astype(jnp.float32)).astype(jnp.bfloat16)


def solve(info, row_map, blocks, rhs):
    vmem = pl.BlockSpec(memory_space=pltpu.VMEM)
    smem = pl.BlockSpec(memory_space=pltpu.SMEM)
    return pl.pallas_call(
        solve_kernel,
        in_specs=[smem, smem, vmem, vmem],
        out_specs=[vmem, vmem, smem],
        out_shape=[jax.ShapeDtypeStruct((K, W), jnp.bfloat16)] * 2 + [jax.ShapeDtypeStruct((4 * HALF,), jnp.int32)],
        scratch_shapes=[
            pltpu.VMEM((K, K + W), jnp.float32),
            pltpu.VMEM((K, B), jnp.float32),
            pltpu.VMEM((K, W), jnp.float32),
        ],
        compiler_params=pltpu.CompilerParams(vmem_limit_bytes=VMEM_LIMIT),
        cost_estimate=pl.CostEstimate(flops=8_000_000_000, bytes_accessed=100_000_000, transcendentals=0),
        name="solve",
    )(info, row_map, blocks, rhs)


def gathered_block(r, b):
    c = r * (HALF // 2) + b // 2
    return jnp.where(b % 2 == 0, c, (3 - c // 16) * 16 + c % 16)


def block(ref, b):
    return ref.at[pl.ds(pl.multiple_of(b * B, B), B), :]


def update_kernel(leaving, info_ref, map_ref, plan_ref, panel_ref, front_ref, hi_ref, lo_ref, *rest):
    if leaving:
        fact_ref, send1_ref, send2_ref = rest[:3]
        rest = rest[3:]
    else:
        fact_ref, parent_ref = rest[1:3]
        rest = rest[3:]
    panel_buf, base_buf, fact_buf, out_buf, in_sem, out_sem = rest
    r, col = info_ref[0], info_ref[1]

    first_entry = 0 if leaving else HALF
    count = plan_ref[3 * HALF + (0 if leaving else 1)]
    steps = (count + GROUP - 1) // GROUP

    def reads(step, j):
        slot = step % SLOTS
        b = plan_ref[first_entry + step * GROUP + j]
        at = pl.ds(j * B, B)
        return (
            pltpu.make_async_copy(block(panel_ref, gathered_block(r, b)), panel_buf.at[slot, at, :], in_sem.at[slot, j, 0]),
            pltpu.make_async_copy(block(front_ref, b), base_buf.at[slot, at, :], in_sem.at[slot, j, 1]),
        )

    def each(step, act):
        for j in range(GROUP):

            @pl.when(step * GROUP + j < count)
            def _():
                act(j)

    def start_reads(step):
        def act(j):
            for copy in reads(step, j):
                copy.start()

        each(step, act)

    def wait_reads(step):
        def act(j):
            for copy in reads(step, j):
                copy.wait()

        each(step, act)

    def writes(step, do):
        slot = step % SLOTS

        def act(j):
            n = step * GROUP + j
            b = plan_ref[first_entry + n]
            at = pl.ds(j * B, B)
            do(pltpu.make_async_copy(fact_buf.at[slot, at, :], block(fact_ref, b), out_sem.at[slot, j, 0]))
            source, sem = out_buf.at[slot, at, :], out_sem.at[slot, j, 1]
            if leaving:

                @pl.when(n < FIRST)
                def _():
                    do(pltpu.make_async_copy(source, block(send1_ref, n), sem))

                @pl.when(n >= FIRST)
                def _():
                    do(pltpu.make_async_copy(source, block(send2_ref, n - FIRST), sem))

            else:
                do(pltpu.make_async_copy(source, block(parent_ref, map_ref[r * HALF + b] - r * HALF), sem))

        each(step, act)

    for ahead in range(SLOTS - 1):

        @pl.when(ahead < steps)
        def _():
            start_reads(ahead)

    @pl.loop(0, steps)
    def _(step):
        slot = step % SLOTS

        @pl.when(step + SLOTS - 1 < steps)
        def _():
            start_reads(step + SLOTS - 1)

        wait_reads(step)

        @pl.when(step >= SLOTS)
        def _():
            writes(step - SLOTS, lambda copy: copy.wait())

        a = panel_buf[slot]
        hi = a.astype(jnp.bfloat16)
        lo = (a - hi.astype(jnp.float32)).astype(jnp.bfloat16)
        product = jnp.dot(hi, hi_ref[...], preferred_element_type=jnp.float32)
        product += jnp.dot(hi, lo_ref[...], preferred_element_type=jnp.float32)
        product += jnp.dot(lo, hi_ref[...], preferred_element_type=jnp.float32)
        lane = lax.broadcasted_iota(jnp.int32, (B, W), 1)
        first = jnp.minimum(2 * col + (lane >= B).astype(jnp.int32), PANELS)
        for j in range(GROUP):
            at = slice(j * B, (j + 1) * B)
            b = r * HALF + plan_ref[first_entry + jnp.minimum(step * GROUP + j, count - 1)]
            base = jnp.where(col < 3, 0.0, base_buf[slot, at, :])
            value = jnp.where(b >= first, base - product[at, :], 0.0)
            fact_buf[slot, at, :] = value
            out_buf[slot, at, :] = jnp.where(col < 3, 0.0, value)
        writes(step, lambda copy: copy.start())

    for behind in range(SLOTS, 0, -1):

        @pl.when(steps >= behind)
        def _():
            writes(steps - behind, lambda copy: copy.wait())


def update(leaving, info, row_map, lists, panel, front, hi, lo, factored=None):
    smem = pl.BlockSpec(memory_space=pltpu.SMEM)
    vmem = pl.BlockSpec(memory_space=pltpu.VMEM)
    hbm = pl.BlockSpec(memory_space=pl.ANY)
    whole = jax.ShapeDtypeStruct(front.shape, jnp.float32)
    if leaving:
        outs = [whole, jax.ShapeDtypeStruct((FIRST * B, W), jnp.float32), jax.ShapeDtypeStruct(((HALF - FIRST) * B, W), jnp.float32)]
        args, aliases = (), {}
    else:
        outs = [whole, whole]
        args, aliases = (factored,), {7: 0}
    return pl.pallas_call(
        functools.partial(update_kernel, leaving),
        in_specs=[smem, smem, smem, hbm, hbm, vmem, vmem] + [hbm] * len(args),
        out_specs=[hbm] * len(outs),
        out_shape=outs,
        input_output_aliases=aliases,
        scratch_shapes=[
            pltpu.VMEM((SLOTS, GROUP * B, K), jnp.float32),
            pltpu.VMEM((SLOTS, GROUP * B, W), jnp.float32),
            pltpu.VMEM((SLOTS, GROUP * B, W), jnp.float32),
            pltpu.VMEM((SLOTS, GROUP * B, W), jnp.float32),
            pltpu.SemaphoreType.DMA((SLOTS, GROUP, 2)),
            pltpu.SemaphoreType.DMA((SLOTS, GROUP, 2)),
        ],
        compiler_params=pltpu.CompilerParams(vmem_limit_bytes=VMEM_LIMIT),
        cost_estimate=pl.CostEstimate(flops=4_800_000_000, bytes_accessed=32_000_000, transcendentals=0),
        name="update_leaving" if leaving else "update_staying",
    )(info, row_map, lists, panel, front, hi, lo, *args)


def place_kernel(plan_ref, got1_ref, got2_ref, _, parent_ref, buf, in_sem, out_sem):
    count = plan_ref[3 * HALF + 2]

    def read(i):
        rows = CHUNK * B
        source, at = (got1_ref, i) if i * CHUNK < FIRST else (got2_ref, i - FIRST // CHUNK)
        return pltpu.make_async_copy(source.at[pl.ds(at * rows, rows), :], buf.at[pl.ds(i * rows, rows), :], in_sem.at[i])

    def write(n):
        return pltpu.make_async_copy(block(buf, n), block(parent_ref, plan_ref[2 * HALF + n]), out_sem.at[n])

    for i in range(HALF // CHUNK):

        @pl.when(i * CHUNK < count)
        def _():
            read(i).start()

    for i in range(HALF // CHUNK):

        @pl.when(i * CHUNK < count)
        def _():
            read(i).wait()

            @pl.loop(i * CHUNK, jnp.minimum(count, (i + 1) * CHUNK))
            def _(n):
                write(n).start()

    @pl.loop(0, count)
    def _(n):
        write(n).wait()


def place_received(lists, got1, got2, parent):
    smem = pl.BlockSpec(memory_space=pltpu.SMEM)
    hbm = pl.BlockSpec(memory_space=pl.ANY)
    return pl.pallas_call(
        place_kernel,
        in_specs=[smem, hbm, hbm, hbm],
        out_specs=hbm,
        out_shape=jax.ShapeDtypeStruct(parent.shape, jnp.float32),
        input_output_aliases={3: 0},
        scratch_shapes=[
            pltpu.VMEM((HALF * B, W), jnp.float32),
            pltpu.SemaphoreType.DMA((HALF // CHUNK,)),
            pltpu.SemaphoreType.DMA((HALF,)),
        ],
        compiler_params=pltpu.CompilerParams(vmem_limit_bytes=VMEM_LIMIT),
        name="place_received",
    )(lists, got1, got2, parent)


def per_device(front, row_map):
    r, c = lax.axis_index("row"), lax.axis_index("col")
    y, z, x = c // 16, c // 4 % 4, c % 4
    info = jnp.stack([r, c]).astype(jnp.int32)

    top, top_half = transposed_top(front)
    cross = send(
        top_half,
        [((0, k), (int(place(k)[0] >= 2), mirror(k))) for k in range(COLS)],
    )
    down = send(top, [((0, k), (1, k)) for k in range(COLS)])
    mine = jnp.where(r == 0, top, down)
    piece = jnp.where((y >= 2) == (r == 1), mine[:B], cross)
    panel = lax.all_gather(piece, "col", axis=0, tiled=True)

    top, front_top, _ = lax.optimization_barrier((top, front[:K], piece))
    diag = jnp.where(c == 0, front_top[:W], jnp.where(c == 1, front_top[W : 2 * W], front_top[2 * W :]))
    off = jnp.where(c == 0, top[:, W : 2 * W], jnp.where(c == 1, top[:, 2 * W :], front_top[:W]))
    owners = [0, 1, 2]
    diag = spread(diag, 1, owners, z)
    off = spread(off, 0, owners, y)
    diag = spread(diag, 0, [k for k in range(COLS) if place(k)[0] == 0 and k % 4 < 3], y)
    off = spread(off, 1, [k for k in range(COLS) if place(k)[1] == 0 and k % 4 < 3], z)
    own = jnp.concatenate([diag, off], 0)
    near = {0: own}
    for d in (1, -1):
        near[d % 4] = send(own, [((0, k), (0, moved(k, 2, d))) for k in range(COLS) if k % 4 < 3])
    halves = [
        send(near[1][:W], [((0, moved(k, 2, 1)), (0, moved(k, 2, 2))) for k in range(COLS) if k % 4 < 3]),
        send(near[3][W:], [((0, moved(k, 2, -1)), (0, moved(k, 2, -2))) for k in range(COLS) if k % 4 < 3]),
    ]
    near[2] = jnp.concatenate(halves, 0)
    blocks = []
    for j in range(3):
        d = (x - j) % 4
        blocks.append(jnp.where(d == 0, near[0], jnp.where(d == 1, near[1], jnp.where(d == 2, near[2], near[3]))))
    blocks = jnp.stack(blocks)
    blocks_down = send(blocks, [((0, k), (1, k)) for k in range(COLS)])
    blocks = jnp.where(r == 0, blocks, blocks_down)
    hi, lo, lists = solve(info, row_map, blocks, mine)

    many = jnp.sum((row_map[:HALF] >= HALF).astype(jnp.int32)) > FIRST
    hi, many = lax.optimization_barrier((hi, many))
    factored, send1, send2 = update(True, info, row_map, lists, panel, front, hi, lo)
    swap = [((i, k), (1 - i, k)) for i in range(2) for k in range(COLS)]
    got1 = send(send1, swap)
    factored, parent = update(False, info, row_map, lists, panel, front, hi, lo, factored)
    got2 = lax.cond(many, lambda v: send(v, swap), lambda v: v, send2)
    parent = place_received(lists, got1, got2, parent)
    return factored, parent


def solution(mesh):
    return jax.shard_map(
        per_device,
        mesh=mesh,
        in_specs=(P("row", "col"), P()),
        out_specs=(P("row", "col"), P("row", "col")),
        check_vma=False,
    )
```
